32 devices in a mesh: vox: 2 (over x), row: 4 (over z), wl: 4 (over y, core).
Axes of the slice: x: 2, y: 2, z: 4, core: 2. Of those that a mesh axis runs over, the one named last changes fastest.
Arguments:
- jacobian: bfloat16 [2048, 1280], P(('row', 'wl'), 'vox'), may hold values from -0.15625 to 0.15625
- extinction: float32 [4, 2], replicated, may hold values from 0.3 to 3
- prior_var: float32 [2, 1280], P(None, 'vox'), may hold values from 0.1 to 10
Outputs:
- gram: float32 [2048, 2048], P(('row', 'wl'), 'vox')
The draws below stay inside these ranges and needn't reach their ends.
All inputs are finite; a program needn't handle non-finite values.
Results may differ from the reference program's by a relative error of at most 0.005.
Values may be sent and summed in bfloat16 or wider, within the bound.
No kernel may reach another device: no remote copies, remote signals or barrier semaphores. Data moves between devices by JAX's collectives and lax.ppermute only.
A program may use at most 128 MiB of HBM per device.

```python
import math
import jax
import jax.numpy as jnp
from jax import lax

WL = 4
CHROM = 2
ROW_DEV = 128
GRAM = 2048
VOX = 1280


def levels(rng, shape, cuts, smallest, high):
    def one(axis_at, parts):
        draws = jax.random.uniform(jax.random.fold_in(jax.random.fold_in(rng, 6), axis_at), (parts,), jnp.float32, smallest / len(cuts), high / len(cuts))
        return jnp.repeat(jnp.exp(draws), shape[axis_at] // parts).reshape((-1,) + (1,) * (len(shape) - axis_at - 1))

    level = one(*cuts[0])
    for cut in cuts[1:]:
        level = level * one(*cut)
    return level


def gaussian(stream_key, shape, scale, limit, split=(), held_as=jnp.bfloat16):
    entries = jax.random.normal(stream_key, shape, jnp.float32) * scale
    if len(split) > 0:
        entries = levels(stream_key, shape, split, -0.22, 0.18) * entries
    return jnp.clip(entries, min=-limit, max=limit).astype(held_as)


def setup_inputs(seed: int = 0) -> dict:
    keys = jax.random.split(jax.random.key(seed), 4)
    jacobian = gaussian(keys[0], (GRAM, VOX), VOX ** -0.5, 0.15625, ((0, 16), (1, 2)))
    extinction = jnp.clip(jnp.exp(jax.random.uniform(keys[1], (WL, CHROM), jnp.float32, math.log(0.3), math.log(3.0))), 0.3, 3.0)
    prior_var = jnp.clip(jnp.exp(math.log(10.0) - 4.6051702 * jax.random.uniform(keys[2], (CHROM, VOX), jnp.float32) ** levels(keys[2], (CHROM, VOX), ((1, 2),), -0.2, 0.2)), 0.1, 10.0)
    return dict(jacobian=jacobian, extinction=extinction, prior_var=prior_var)


def reference(jacobian, extinction, prior_var):
    order = jacobian.shape[0]
    voxels = jacobian.shape[1]
    tiles = order // (ROW_DEV * WL)
    waves = (jnp.arange(order, dtype=jnp.int32) // ROW_DEV) % WL
    jac_wide = jacobian.astype(jnp.float32)
    result = jnp.zeros((tiles, WL, ROW_DEV, order), jnp.float32)
    for wave_index in range(WL):
        table = jnp.dot(extinction * extinction[wave_index][None, :], prior_var, precision=lax.Precision.HIGHEST)
        weights = table[waves]
        scaled = jac_wide * weights
        picked = jac_wide.reshape(tiles, WL, ROW_DEV, voxels)[:, wave_index].reshape(tiles * ROW_DEV, voxels)
        block_rows = jnp.dot(picked, scaled.T, precision=lax.Precision.HIGHEST, preferred_element_type=jnp.float32)
        result = result.at[:, wave_index].set(block_rows.reshape(tiles, ROW_DEV, order))
    return jnp.tril(result.reshape(order, order))
```

```python
import functools

import jax
import jax.numpy as jnp
import numpy as np
from jax import lax
from jax.experimental import pallas as pl
from jax.experimental.pallas import tpu as pltpu
from jax.sharding import PartitionSpec as P


def shift(x, axis, by):
    size = lax.axis_size(axis)
    return lax.ppermute(x, axis, [(i, (i + by) % size) for i in range(size)])


def swap(x, axis, bit):
    size = lax.axis_size(axis)
    return lax.ppermute(x, axis, [(i, i ^ bit) for i in range(size)])


def plan(vox, levels):
    slots = levels // vox
    ready = [0, 1] + list(range(3, levels + 1))
    ready[levels - 1] = 2
    slot = np.zeros((vox, levels, slots), np.int32)
    dist = np.zeros((vox, levels, slots), np.int32)
    for v in range(vox):
        for z in range(levels):
            ds = [z - (v * slots + s) for s in range(slots)]
            order = sorted(range(slots), key=lambda s: (ready[max(ds[s], 0)], s))
            slot[v, z] = order
            dist[v, z] = [max(ds[s], 0) for s in order]
    return slot, dist


def pick(pieces, dist, v, z, phase):
    here = jnp.asarray(dist[:, :, phase])[v, z]
    used = sorted(set(dist[:, :, phase].ravel().tolist()))
    out = pieces[used[0]]
    for d in used[1:]:
        out = jnp.where(here == d, pieces[d], out)
    return out


def place_kernel(count, where_ref, *refs):
    blocks, out_ref = refs[:count], refs[count]
    tile = blocks[0].shape[0]
    rows = where_ref[count] + lax.broadcasted_iota(jnp.int32, (tile, tile), 0)
    for k in range(count):
        at = pl.multiple_of(where_ref[k] * tile, tile)
        cols = where_ref[count + 1] + at + lax.broadcasted_iota(jnp.int32, (tile, tile), 1)
        out_ref[:, pl.ds(at, tile)] = jnp.where(cols <= rows, blocks[k][...], 0.0)


def place(blocks, where):
    tile = blocks[0].shape[0]
    return pl.pallas_call(
        functools.partial(place_kernel, len(blocks)),
        out_shape=jax.ShapeDtypeStruct((tile, tile * len(blocks)), jnp.float32),
        in_specs=[pl.BlockSpec(memory_space=pltpu.SMEM)]
        + [pl.BlockSpec(memory_space=pltpu.VMEM)] * len(blocks),
        out_specs=pl.BlockSpec(memory_space=pltpu.VMEM),
    )(where, *blocks)


def on_device(jac, extinction, prior_var):
    tile = jac.shape[0]
    vox, levels, lines = (lax.axis_size(a) for a in ("vox", "row", "wl"))
    v, z, w = (lax.axis_index(a) for a in ("vox", "row", "wl"))
    slots = levels // vox
    slot, dist = plan(vox, levels)

    pieces = {0: jac}
    for d in [1, levels - 1] + list(range(2, levels - 1)):
        if d not in pieces and d > 0:
            near = d in (1, levels - 1)
            pieces[d] = shift(jac if near else pieces[d - 1], "row", d if near else 1)

    halves = [jac] + [shift(jac, "vox", -t) for t in range(1, vox)]
    priors = [prior_var] + [shift(prior_var, "vox", -t) for t in range(1, vox)]
    rows = []
    for half in halves:
        got = {0: half}
        bit = lines // 2
        while bit:
            got.update({d ^ bit: swap(x, "wl", bit) for d, x in list(got.items())})
            bit //= 2
        rows.append(got)

    waves = extinction.shape[0]
    mine = extinction[w % waves]
    high, low = [], []
    for t in range(vox):
        for d in range(lines):
            coeff = extinction[(w ^ d) % waves] * mine
            weight = jnp.sum(coeff[:, None] * priors[t], axis=0)
            scaled = rows[t][d].astype(jnp.float32) * weight[None, :]
            top = lax.reduce_precision(scaled, 8, 7)
            high.append(top.astype(jnp.bfloat16))
            low.append((scaled - top).astype(jnp.bfloat16))

    blocks, where = [], []
    for phase in range(slots):
        total = None
        for t in range(vox):
            if t == 0:
                cols = pick(pieces, dist, v, z, phase)
            else:
                cols = pick(pieces, dist, (v - t) % vox, z, phase)
                cols = shift(cols, "vox", -t)
            for part in (high, low):
                left = jnp.concatenate(part[t * lines : (t + 1) * lines], axis=0)
                term = lax.dot_general(
                    left, cols, (((1,), (1,)), ((), ())), preferred_element_type=jnp.float32
                )
                total = term if total is None else total + term
        for d in range(lines):
            block = total[d * tile : (d + 1) * tile]
            blocks.append(block if d == 0 else swap(block, "wl", d))
            where.append(jnp.asarray(slot[:, :, phase])[v, z] * lines + (w ^ d))
    where += [(z * lines + w) * tile, v * slots * lines * tile]
    return place(blocks, jnp.stack(where).astype(jnp.int32))


def solution(mesh):
    return jax.shard_map(
        on_device,
        mesh=mesh,
        in_specs=(P(("row", "wl"), "vox"), P(), P(None, "vox")),
        out_specs=P(("row", "wl"), "vox"),
        check_vma=False,
    )
```

```python
import functools

import jax
import jax.numpy as jnp
from jax import lax
from jax.experimental import pallas as pl
from jax.experimental.pallas import tpu as pltpu
from jax.sharding import PartitionSpec as P

VMEM = pl.BlockSpec(memory_space=pltpu.VMEM)
LIMIT = 16 * 2**20
SMEM = pl.BlockSpec(memory_space=pltpu.SMEM)


def shift(x, axis, by):
    size = lax.axis_size(axis)
    return lax.ppermute(x, axis, [(i, (i + by) % size) for i in range(size)])


def swap(x, axis, bit):
    size = lax.axis_size(axis)
    return lax.ppermute(x, axis, [(i, i ^ bit) for i in range(size)])


def ready(dist, levels):
    return jnp.where(dist <= 1, dist, jnp.where(dist == levels - 1, 2, dist + 1))


def choose(vox, level, phase, slots, levels):
    dists = [jnp.maximum(level - (vox * slots + s), 0) for s in range(slots)]
    keys = [ready(d, levels) for d in dists]
    slot = dist = jnp.int32(0)
    for s in range(slots):
        rank = jnp.int32(0)
        for o in range(slots):
            if o != s:
                first = keys[o] <= keys[s] if o < s else keys[o] < keys[s]
                rank += first.astype(jnp.int32)
        slot = jnp.where(rank == phase, s, slot)
        dist = jnp.where(rank == phase, dists[s], dist)
    return slot, dist


def used(phase, slots, levels):
    out = set()
    rank = lambda d: d if d <= 1 else 2 if d == levels - 1 else d + 1
    for v in range(levels // slots):
        for z in range(levels):
            ds = [max(z - (v * slots + s), 0) for s in range(slots)]
            out.add(sorted(ds, key=rank)[phase])
    return sorted(out)


def pick_kernel(phase, slots, levels, vox, dists, *refs):
    pieces, outs = refs[: len(dists)], refs[len(dists) :]
    v, z = lax.axis_index("vox"), lax.axis_index("row")
    for t, out in enumerate(outs):
        _, dist = choose(lax.rem(v + vox - t, vox), z, phase, slots, levels)
        for d, piece in zip(dists, pieces):

            @pl.when(dist == d)
            def _():
                out[...] = piece[...]


def pick(pieces, phase, slots, levels, vox):
    dists = used(phase, slots, levels)
    like = jax.ShapeDtypeStruct(pieces[0].shape, pieces[0].dtype)
    return pl.pallas_call(
        functools.partial(pick_kernel, phase, slots, levels, vox, dists),
        out_shape=[like] * vox,
        compiler_params=pltpu.CompilerParams(vmem_limit_bytes=LIMIT),
        in_specs=[VMEM] * len(dists),
        out_specs=[VMEM] * vox,
    )(*[pieces[d] for d in dists])


def weigh_kernel(vox, lines, extinction_ref, *refs):
    priors, rows, (high_ref, low_ref) = refs[:vox], refs[vox:-2], refs[-2:]
    waves, chroms = extinction_ref.shape
    tile = rows[0].shape[0]
    w = lax.axis_index("wl")
    for t in range(vox):
        for d in range(lines):
            weight = 0.0
            for c in range(chroms):
                coeff = extinction_ref[lax.rem(w ^ d, waves), c] * extinction_ref[lax.rem(w, waves), c]
                weight += coeff * priors[t][c : c + 1, :]
            scaled = rows[t * lines + d][...].astype(jnp.float32) * weight
            top = scaled.astype(jnp.bfloat16)
            high_ref[t, d * tile : (d + 1) * tile, :] = top
            low_ref[t, d * tile : (d + 1) * tile, :] = (scaled - top.astype(jnp.float32)).astype(jnp.bfloat16)


def weigh(extinction, priors, rows):
    vox, lines = len(rows), len(rows[0])
    tile, depth = rows[0][0].shape
    like = jax.ShapeDtypeStruct((vox, lines * tile, depth), jnp.bfloat16)
    flat = [rows[t][d] for t in range(vox) for d in range(lines)]
    return pl.pallas_call(
        functools.partial(weigh_kernel, vox, lines),
        out_shape=[like, like],
        compiler_params=pltpu.CompilerParams(vmem_limit_bytes=LIMIT),
        in_specs=[SMEM] + [VMEM] * (vox + len(flat)),
        out_specs=[VMEM, VMEM],
    )(extinction, *priors, *flat)


def multiply_kernel(vox, high_ref, low_ref, *refs):
    cols, outs = refs[:vox], refs[vox:]
    tile = cols[0].shape[0]
    total = 0.0
    for t in range(vox):
        for part in (high_ref, low_ref):
            total += lax.dot_general(
                part[t], cols[t][...], (((1,), (1,)), ((), ())), preferred_element_type=jnp.float32
            )
    for d, out in enumerate(outs):
        out[...] = total[d * tile : (d + 1) * tile]


def multiply(high, low, cols, lines):
    vox, tile = len(cols), cols[0].shape[0]
    like = jax.ShapeDtypeStruct((tile, tile), jnp.float32)
    return pl.pallas_call(
        functools.partial(multiply_kernel, vox),
        out_shape=[like] * lines,
        compiler_params=pltpu.CompilerParams(vmem_limit_bytes=LIMIT),
        in_specs=[VMEM] * (2 + vox),
        out_specs=[VMEM] * lines,
    )(high, low, *cols)


def place_kernel(slots, lines, levels, *refs):
    blocks, out_ref = refs[:-1], refs[-1]
    tile = blocks[0].shape[0]
    v, z, w = (lax.axis_index(a) for a in ("vox", "row", "wl"))
    rows = (z * lines + w) * tile + lax.broadcasted_iota(jnp.int32, (tile, tile), 0)
    for p in range(slots):
        slot, _ = choose(v, z, p, slots, levels)
        for d in range(lines):
            at = pl.multiple_of((slot * lines + (w ^ d)) * tile, tile)
            cols = v * (slots * lines * tile) + at + lax.broadcasted_iota(jnp.int32, (tile, tile), 1)
            out_ref[:, pl.ds(at, tile)] = jnp.where(cols <= rows, blocks[p * lines + d][...], 0.0)


def place(blocks, slots, lines, levels):
    tile = blocks[0].shape[0]
    return pl.pallas_call(
        functools.partial(place_kernel, slots, lines, levels),
        out_shape=jax.ShapeDtypeStruct((tile, tile * len(blocks)), jnp.float32),
        compiler_params=pltpu.CompilerParams(vmem_limit_bytes=LIMIT),
        in_specs=[VMEM] * len(blocks),
        out_specs=VMEM,
    )(*blocks)


def on_device(jac, extinction, prior_var):
    vox, levels, lines = (lax.axis_size(a) for a in ("vox", "row", "wl"))
    slots = levels // vox

    pieces = {0: jac}
    for d in [1, levels - 1] + list(range(2, levels - 1)):
        if d not in pieces and d > 0:
            near = d in (1, levels - 1)
            pieces[d] = shift(jac if near else pieces[d - 1], "row", d if near else 1)

    halves = [jac] + [shift(jac, "vox", -t) for t in range(1, vox)]
    priors = [prior_var] + [shift(prior_var, "vox", -t) for t in range(1, vox)]
    rows = []
    for half in halves:
        got = {0: half}
        bit = lines // 2
        while bit:
            got.update({d ^ bit: swap(x, "wl", bit) for d, x in list(got.items())})
            bit //= 2
        rows.append([got[d] for d in range(lines)])
    high, low = weigh(extinction, priors, rows)

    blocks = []
    for phase in range(slots):
        cols = pick(pieces, phase, slots, levels, vox)
        cols = [cols[0]] + [shift(cols[t], "vox", -t) for t in range(1, vox)]
        done = multiply(high, low, cols, lines)
        blocks += [done[0]] + [swap(done[d], "wl", d) for d in range(1, lines)]
    return place(blocks, slots, lines, levels)


def solution(mesh):
    return jax.shard_map(
        on_device,
        mesh=mesh,
        in_specs=(P(("row", "wl"), "vox"), P(), P(None, "vox")),
        out_specs=P(("row", "wl"), "vox"),
        check_vma=False,
    )
```

```python
import functools

import jax
import jax.numpy as jnp
from jax import lax
from jax.experimental import pallas as pl
from jax.experimental.pallas import tpu as pltpu
from jax.sharding import PartitionSpec as P

LIMIT = 16 * 2**20
EXTRA = 16
SMEM = pl.BlockSpec(memory_space=pltpu.SMEM)
VMEM = pl.BlockSpec(memory_space=pltpu.VMEM)


def shift(x, axis, by):
    size = lax.axis_size(axis)
    return lax.ppermute(x, axis, [(i, (i + by) % size) for i in range(size)])


def swap(x, axis, bit):
    size = lax.axis_size(axis)
    return lax.ppermute(x, axis, [(i, i ^ bit) for i in range(size)])


def send(x, by, bit):
    vox, lines = lax.axis_size("vox"), lax.axis_size("wl")
    pairs = [
        (v * lines + w, (v + by) % vox * lines + (w ^ bit)) for v in range(vox) for w in range(lines)
    ]
    return lax.ppermute(x, ("vox", "wl"), pairs)


def kernel_call(kernel, ins, outs, scratch=()):
    return functools.partial(
        pl.pallas_call,
        kernel,
        in_specs=ins,
        out_specs=[VMEM] * len(outs),
        out_shape=outs,
        scratch_shapes=scratch,
        compiler_params=pltpu.CompilerParams(vmem_limit_bytes=LIMIT),
    )()


def weigh_kernel(far, near, extinction_ref, prior_ref, *refs):
    rows, (high_ref, low_ref) = refs[:-2], refs[-2:]
    chroms, waves = extinction_ref.shape
    tile = rows[0].shape[0]
    w = lax.axis_index("wl")
    for i, e in enumerate(near):
        for j, f in enumerate(far):
            weight = 0.0
            for c in range(chroms):
                coeff = extinction_ref[c, lax.rem(w ^ f, waves)] * extinction_ref[c, lax.rem(w ^ e, waves)]
                weight += coeff * prior_ref[c : c + 1, :]
            scaled = rows[j][...].astype(jnp.float32) * weight
            top = scaled.astype(jnp.bfloat16)
            high_ref[i, j * tile : (j + 1) * tile, :] = top
            low_ref[i, j * tile : (j + 1) * tile, :] = (scaled - top.astype(jnp.float32)).astype(jnp.bfloat16)


def weigh(extinction, prior, rows, far, near):
    tile, depth = rows[0].shape
    like = jax.ShapeDtypeStruct((len(near), len(far) * tile, depth), jnp.bfloat16)
    call = kernel_call(
        functools.partial(weigh_kernel, far, near), [SMEM] + [VMEM] * (1 + len(rows)), [like, like]
    )
    return call(extinction, prior, *rows)


def multiply_kernel(vox, levels, far, near, high_ref, low_ref, *refs):
    count = levels * len(near)
    pieces, outs, cols_ref = refs[:count], refs[count:-1], refs[-1]
    tile, slots = pieces[0].shape[0], levels // vox
    v, z = lax.axis_index("vox"), lax.axis_index("row")
    for t in range(vox):
        owner = lax.rem(v + t, vox)
        for s in range(slots):
            dist = jnp.maximum(z - (owner * slots + s), 0)
            at = (t * slots + s) * tile
            for d in range(levels):

                @pl.when(dist == d)
                def _():
                    for i in range(len(near)):
                        cols_ref[i, at : at + tile] = pieces[d * len(near) + i][...]

    for i in range(len(near)):
        total = 0.0
        for part in (high_ref, low_ref):
            total += lax.dot_general(
                part[i], cols_ref[i], (((1,), (1,)), ((), ())), preferred_element_type=jnp.float32
            )
        for t in range(vox):
            for j in range(len(far)):
                for s in range(slots):
                    to, at = (s * len(near) + i) * tile, (t * slots + s) * tile
                    outs[t * len(far) + j][:tile, to : to + tile] = total[
                        j * tile : (j + 1) * tile, at : at + tile
                    ]
    for out in outs[1:]:
        largest = jnp.max(jnp.abs(out[:tile]), axis=(0, 1), keepdims=True)
        power = jnp.floor(jnp.log2(jnp.maximum(largest, 1e-30))) - 13.0
        out[:tile] *= jnp.exp2(-power)
        out[tile:] = jnp.broadcast_to(power, out[tile:].shape)


def multiply(high, low, pieces, vox, far, near):
    levels = len(pieces)
    tile, depth = pieces[0][0].shape
    width = levels // vox * len(near) * tile
    flat = [pieces[d][i] for d in range(levels) for i in range(len(near))]
    call = kernel_call(
        functools.partial(multiply_kernel, vox, levels, far, near),
        [VMEM] * (2 + len(flat)),
        [jax.ShapeDtypeStruct((tile + (EXTRA if k else 0), width), jnp.float32) for k in range(vox * len(far))],
        [pltpu.VMEM((len(near), levels * tile, depth), jnp.bfloat16)],
    )
    return call(high, low, *flat)


def place_kernel(vox, slots, lines, far, near, *refs):
    blocks, out_ref = refs[:-1], refs[-1]
    tile = out_ref.shape[0]
    v, z, w = (lax.axis_index(a) for a in ("vox", "row", "wl"))
    rows = (z * lines + w) * tile + lax.broadcasted_iota(jnp.int32, (tile, tile), 0)
    for j, f in enumerate(far):
        for s in range(slots):
            for i, e in enumerate(near):
                src = slice((s * len(near) + i) * tile, (s * len(near) + i + 1) * tile)
                total = 0.0
                for t in range(vox):
                    block = blocks[t * len(far) + j]
                    scale = 1.0 if t == j == 0 else jnp.exp2(block[tile : tile + 1, :1])
                    total += block[:tile, src] * scale
                at = pl.multiple_of((s * lines + (w ^ f ^ e)) * tile, tile)
                cols = v * (slots * lines * tile) + at + lax.broadcasted_iota(jnp.int32, (tile, tile), 1)
                out_ref[:, pl.ds(at, tile)] = jnp.where(cols <= rows, total, 0.0)


def place(blocks, vox, slots, lines, far, near):
    tile = blocks[0].shape[0]
    call = kernel_call(
        functools.partial(place_kernel, vox, slots, lines, far, near),
        [VMEM] * len(blocks),
        [jax.ShapeDtypeStruct((tile, slots * lines * tile), jnp.float32)],
    )
    return call(*blocks)[0]


def on_device(jac, extinction, prior_var):
    vox, levels, lines = (lax.axis_size(a) for a in ("vox", "row", "wl"))
    slots = levels // vox
    far = [0, lines // 2] if lines > 1 else [0]
    near = list(range(max(lines // 2, 1)))

    rows = [jac] + [swap(jac, "wl", f) for f in far[1:]]

    below = {0: jac}
    for d in [1, levels - 1] + list(range(2, levels - 1)):
        if d not in below and d > 0:
            direct = d in (1, levels - 1)
            if d == 2:
                below[1], *rows[1:] = lax.optimization_barrier([below[1]] + rows[1:])
            below[d] = shift(jac if direct else below[d - 1], "row", d if direct else 1)
    high, low = weigh(extinction.T, prior_var, rows, far, near)
    for d in range(2, levels - 1):
        below[d], high, low = lax.optimization_barrier([below[d], high, low])
    pieces = [[below[d]] + [swap(below[d], "wl", e) for e in near[1:]] for d in range(levels)]

    shares = multiply(high, low, pieces, vox, far, near)
    blocks = []
    for t in range(vox):
        for j, f in enumerate(far):
            share = shares[t * len(far) + j]
            if t or f:
                share = send(share.astype(jnp.float16), t, f).astype(jnp.float32)
            blocks.append(share)
    return place(blocks, vox, slots, lines, far, near)


def solution(mesh):
    return jax.shard_map(
        on_device,
        mesh=mesh,
        in_specs=(P(("row", "wl"), "vox"), P(), P(None, "vox")),
        out_specs=P(("row", "wl"), "vox"),
        check_vma=False,
    )
```

```python
import functools

import jax
import jax.numpy as jnp
from jax import lax
from jax.experimental import pallas as pl
from jax.experimental.pallas import tpu as pltpu
from jax.sharding import PartitionSpec as P

LIMIT = 16 * 2**20
EXTRA = 16
SMEM = pl.BlockSpec(memory_space=pltpu.SMEM)
VMEM = pl.BlockSpec(memory_space=pltpu.VMEM)


def shift(x, axis, by):
    size = lax.axis_size(axis)
    return lax.ppermute(x, axis, [(i, (i + by) % size) for i in range(size)])


def climb(x, by, lowest, count):
    return lax.ppermute(x, "row", [(i - by, i) for i in range(lowest, lowest + count)])


def swap(x, axis, bit):
    size = lax.axis_size(axis)
    return lax.ppermute(x, axis, [(i, i ^ bit) for i in range(size)])


def send(x, by, bit):
    vox, lines = lax.axis_size("vox"), lax.axis_size("wl")
    pairs = [
        (v * lines + w, (v + by) % vox * lines + (w ^ bit)) for v in range(vox) for w in range(lines)
    ]
    return lax.ppermute(x, ("vox", "wl"), pairs)


def kernel_call(kernel, ins, outs, scratch=()):
    return functools.partial(
        pl.pallas_call,
        kernel,
        in_specs=ins,
        out_specs=[VMEM] * len(outs),
        out_shape=outs,
        scratch_shapes=scratch,
        compiler_params=pltpu.CompilerParams(vmem_limit_bytes=LIMIT),
    )()


def ready(dist, levels):
    return jnp.where(dist <= 1, dist, jnp.where(dist == levels - 1, 2, dist + 1))


def choose(vox, level, phase, slots, levels):
    dists = [jnp.maximum(level - (vox * slots + s), 0) for s in range(slots)]
    keys = [ready(d, levels) for d in dists]
    slot = dist = jnp.int32(0)
    for s in range(slots):
        rank = jnp.int32(0)
        for o in range(slots):
            if o != s:
                first = keys[o] <= keys[s] if o < s else keys[o] < keys[s]
                rank += first.astype(jnp.int32)
        slot = jnp.where(rank == phase, s, slot)
        dist = jnp.where(rank == phase, dists[s], dist)
    return slot, dist


def used(phase, slots, levels):
    out = set()
    rank = lambda d: d if d <= 1 else 2 if d == levels - 1 else d + 1
    for v in range(levels // slots):
        for z in range(levels):
            ds = [max(z - (v * slots + s), 0) for s in range(slots)]
            out.add(sorted(ds, key=rank)[phase])
    return sorted(out)


def prepare_kernel(far, near, extinction_ref, prior_ref, jac_ref, weights_ref, own_ref):
    chroms, waves = extinction_ref.shape
    w = lax.axis_index("wl")
    for i, e in enumerate(near):
        for j, f in enumerate(far):
            weight = 0.0
            for c in range(chroms):
                coeff = extinction_ref[c, lax.rem(w ^ f, waves)] * extinction_ref[c, lax.rem(w ^ e, waves)]
                weight += coeff * prior_ref[c : c + 1, :]
            weights_ref[i * len(far) + j : i * len(far) + j + 1, :] = weight
    own_ref[...] = jac_ref[...]


def prepare(extinction, prior, jac, far, near):
    weights = jax.ShapeDtypeStruct((len(far) * len(near), jac.shape[1]), jnp.float32)
    own = jax.ShapeDtypeStruct(jac.shape, jac.dtype)
    call = kernel_call(functools.partial(prepare_kernel, far, near), [SMEM, VMEM, VMEM], [weights, own])
    return call(extinction, prior, jac)


def weigh_kernel(far, near, weights_ref, *refs):
    rows, (high_ref, low_ref) = refs[:-2], refs[-2:]
    tile = rows[0].shape[0]
    for i in range(len(near)):
        for j in range(len(far)):
            k = i * len(far) + j
            scaled = rows[j][...].astype(jnp.float32) * weights_ref[k : k + 1, :]
            top = scaled.astype(jnp.bfloat16)
            high_ref[i, j * tile : (j + 1) * tile, :] = top
            low_ref[i, j * tile : (j + 1) * tile, :] = (scaled - top.astype(jnp.float32)).astype(jnp.bfloat16)


def weigh(weights, rows, far, near):
    tile, depth = rows[0].shape
    like = jax.ShapeDtypeStruct((len(near), len(far) * tile, depth), jnp.bfloat16)
    call = kernel_call(functools.partial(weigh_kernel, far, near), [VMEM] * (1 + len(rows)), [like, like])
    return call(weights, *rows)


def multiply_kernel(vox, levels, phases, dists, far, near, high_ref, low_ref, *refs):
    count = len(dists) * len(near)
    pieces, outs, cols_ref = refs[:count], refs[count:-1], refs[-1]
    tile = pieces[0].shape[0]
    v, z = lax.axis_index("vox"), lax.axis_index("row")
    parts = [(t, p) for t in range(vox) for p in range(len(phases))]
    for n, (t, p) in enumerate(parts):
        _, dist = choose(lax.rem(v + t, vox), z, phases[p], levels // vox, levels)
        for k, d in enumerate(dists):

            @pl.when(dist == d)
            def _():
                for i in range(len(near)):
                    cols_ref[i, n * tile : (n + 1) * tile] = pieces[k * len(near) + i][...]

    for i in range(len(near)):
        total = 0.0
        for part in (high_ref, low_ref):
            total += lax.dot_general(
                part[i], cols_ref[i], (((1,), (1,)), ((), ())), preferred_element_type=jnp.float32
            )
        for n, (t, p) in enumerate(parts):
            to = (p * len(near) + i) * tile
            for j in range(len(far)):
                outs[t * len(far) + j][:tile, to : to + tile] = total[
                    j * tile : (j + 1) * tile, n * tile : (n + 1) * tile
                ]
    for out in outs[1:]:
        largest = jnp.max(jnp.abs(out[:tile]), axis=(0, 1), keepdims=True)
        power = jnp.floor(jnp.log2(jnp.maximum(largest, 1e-30))) - 13.0
        out[:tile] *= jnp.exp2(-power)
        out[tile:] = jnp.broadcast_to(power, out[tile:].shape)


def multiply(high, low, pieces, vox, phases, far, near):
    levels = len(pieces)
    tile, depth = pieces[0][0].shape
    dists = sorted(set().union(*[used(p, levels // vox, levels) for p in phases]))
    flat = [pieces[d][i] for d in dists for i in range(len(near))]
    heights = [tile] + [tile + EXTRA] * (vox * len(far) - 1)
    width = len(phases) * len(near) * tile
    call = kernel_call(
        functools.partial(multiply_kernel, vox, levels, phases, dists, far, near),
        [VMEM] * (2 + len(flat)),
        [jax.ShapeDtypeStruct((height, width), jnp.float32) for height in heights],
        [pltpu.VMEM((len(near), vox * len(phases) * tile, depth), jnp.bfloat16)],
    )
    return call(high, low, *flat)


def place_kernel(vox, levels, lines, groups, far, near, *refs):
    blocks, out_ref = refs[:-1], refs[-1]
    tile, slots = out_ref.shape[0], levels // vox
    v, z, w = (lax.axis_index(a) for a in ("vox", "row", "wl"))
    rows = (z * lines + w) * tile + lax.broadcasted_iota(jnp.int32, (tile, tile), 0)
    for g, phases in enumerate(groups):
        for p, phase in enumerate(phases):
            slot, _ = choose(v, z, phase, slots, levels)
            for j, f in enumerate(far):
                for i, e in enumerate(near):
                    src = slice((p * len(near) + i) * tile, (p * len(near) + i + 1) * tile)
                    total = 0.0
                    for t in range(vox):
                        block = blocks[(g * vox + t) * len(far) + j]
                        scale = 1.0 if t == j == 0 else jnp.exp2(block[tile : tile + 1, :1])
                        total += block[:tile, src] * scale
                    at = pl.multiple_of((slot * lines + (w ^ f ^ e)) * tile, tile)
                    cols = v * (slots * lines * tile) + at + lax.broadcasted_iota(jnp.int32, (tile, tile), 1)
                    out_ref[:, pl.ds(at, tile)] = jnp.where(cols <= rows, total, 0.0)


def place(blocks, vox, levels, lines, groups, far, near):
    tile = blocks[0].shape[0]
    call = kernel_call(
        functools.partial(place_kernel, vox, levels, lines, groups, far, near),
        [VMEM] * len(blocks),
        [jax.ShapeDtypeStruct((tile, levels // vox * lines * tile), jnp.float32)],
    )
    return call(*blocks)[0]


def on_device(jac, extinction, prior_var):
    vox, levels, lines = (lax.axis_size(a) for a in ("vox", "row", "wl"))
    slots = levels // vox
    far = [0, lines // 2] if lines > 1 else [0]
    near = list(range(max(lines // 2, 1)))

    groups = [list(range(slots))]

    below = {0: jac}
    if levels > 1:
        below[1] = shift(jac, "row", 1)
    others = [swap(jac, "wl", f) for f in far[1:]]
    if levels > 2:
        below[levels - 1] = climb(jac, levels - 1, levels - 1, 1)
    weights, own = prepare(extinction.T, prior_var, jac, far, near)
    if levels > 1:
        below[1], weights, own = lax.optimization_barrier([below[1], weights, own])
    for d in range(2, levels - 1):
        below[d] = climb(below[d - 1], 1, d, levels - d)
    high, low = weigh(weights, [own] + others, far, near)
    below[0] = own
    for d in range(2, levels - 1):
        below[d], high, low = lax.optimization_barrier([below[d], high, low])
    pieces = [[below[d]] + [swap(below[d], "wl", e) for e in near[1:]] for d in range(levels)]

    blocks = []
    for phases in groups:
        shares = multiply(high, low, pieces, vox, phases, far, near)
        for t in range(vox):
            for j, f in enumerate(far):
                share = shares[t * len(far) + j]
                if t or f:
                    share = send(share.astype(jnp.float16), t, f).astype(jnp.float32)
                blocks.append(share)
    return place(blocks, vox, levels, lines, groups, far, near)


def solution(mesh):
    return jax.shard_map(
        on_device,
        mesh=mesh,
        in_specs=(P(("row", "wl"), "vox"), P(), P(None, "vox")),
        out_specs=P(("row", "wl"), "vox"),
        check_vma=False,
    )
```

```python
import functools

import jax
import jax.numpy as jnp
from jax import lax
from jax.experimental import pallas as pl
from jax.experimental.pallas import tpu as pltpu
from jax.sharding import PartitionSpec as P

LIMIT = 16 * 2**20
EXTRA = 16
SMEM = pl.BlockSpec(memory_space=pltpu.SMEM)
VMEM = pl.BlockSpec(memory_space=pltpu.VMEM)


def shift(x, axis, by):
    size = lax.axis_size(axis)
    return lax.ppermute(x, axis, [(i, (i + by) % size) for i in range(size)])


def climb(x, by, lowest, count):
    return lax.ppermute(x, "row", [(i - by, i) for i in range(lowest, lowest + count)])


def swap(x, axis, bit):
    size = lax.axis_size(axis)
    return lax.ppermute(x, axis, [(i, i ^ bit) for i in range(size)])


def send(x, by, bit):
    vox, lines = lax.axis_size("vox"), lax.axis_size("wl")
    pairs = [
        (v * lines + w, (v + by) % vox * lines + (w ^ bit)) for v in range(vox) for w in range(lines)
    ]
    return lax.ppermute(x, ("vox", "wl"), pairs)


def kernel_call(kernel, ins, outs, scratch=()):
    return functools.partial(
        pl.pallas_call,
        kernel,
        in_specs=ins,
        out_specs=[VMEM] * len(outs),
        out_shape=outs,
        scratch_shapes=scratch,
        compiler_params=pltpu.CompilerParams(vmem_limit_bytes=LIMIT),
    )()


def prepare_kernel(far, near, extinction_ref, prior_ref, jac_ref, weights_ref, own_ref):
    chroms, waves = extinction_ref.shape
    w = lax.axis_index("wl")
    for i, e in enumerate(near):
        for j, f in enumerate(far):
            weight = 0.0
            for c in range(chroms):
                coeff = extinction_ref[c, lax.rem(w ^ f, waves)] * extinction_ref[c, lax.rem(w ^ e, waves)]
                weight += coeff * prior_ref[c : c + 1, :]
            weights_ref[i * len(far) + j : i * len(far) + j + 1, :] = weight
    own_ref[...] = jac_ref[...]


def prepare(extinction, prior, jac, far, near):
    weights = jax.ShapeDtypeStruct((len(far) * len(near), jac.shape[1]), jnp.float32)
    own = jax.ShapeDtypeStruct(jac.shape, jac.dtype)
    call = kernel_call(functools.partial(prepare_kernel, far, near), [SMEM, VMEM, VMEM], [weights, own])
    return call(extinction, prior, jac)


def weigh_kernel(far, near, weights_ref, *refs):
    rows, (high_ref, low_ref) = refs[:-2], refs[-2:]
    tile = rows[0].shape[0]
    for i in range(len(near)):
        for j in range(len(far)):
            k = i * len(far) + j
            scaled = rows[j][...].astype(jnp.float32) * weights_ref[k : k + 1, :]
            top = scaled.astype(jnp.bfloat16)
            high_ref[i, j * tile : (j + 1) * tile, :] = top
            low_ref[i, j * tile : (j + 1) * tile, :] = (scaled - top.astype(jnp.float32)).astype(jnp.bfloat16)


def weigh(weights, rows, far, near):
    tile, depth = rows[0].shape
    like = jax.ShapeDtypeStruct((len(near), len(far) * tile, depth), jnp.bfloat16)
    call = kernel_call(functools.partial(weigh_kernel, far, near), [VMEM] * (1 + len(rows)), [like, like])
    return call(weights, *rows)


def emit(out, total, at):
    tile = total.shape[0]
    if out.shape[0] > tile:
        largest = jnp.max(jnp.abs(total), axis=(0, 1), keepdims=True)
        power = jnp.floor(jnp.log2(jnp.maximum(largest, 1e-30))) - 13.0
        out[tile:, at : at + tile] = jnp.broadcast_to(power, (EXTRA, tile))
        total = total * jnp.exp2(-power)
    out[:tile, at : at + tile] = total


def product(high, low, cols):
    dims = (((1,), (1,)), ((), ()))
    return lax.dot_general(high, cols, dims, preferred_element_type=jnp.float32) + lax.dot_general(
        low, cols, dims, preferred_element_type=jnp.float32
    )


def first_kernel(vox, levels, have, far, near, high_ref, low_ref, *refs):
    pieces = dict(zip(have, refs))
    outs, cols_ref = refs[len(have) : -1], refs[-1]
    tile, slots = refs[0].shape[0], levels // vox
    v, z = lax.axis_index("vox"), lax.axis_index("row")
    parts = [(t, s) for t in range(vox) for s in range(slots)]
    for n, (t, s) in enumerate(parts):
        dist = jnp.maximum(z - (lax.rem(v + t, vox) * slots + s), 0)
        for d in range(levels):

            @pl.when(dist == d)
            def _():
                for i in range(len(near)):
                    if (d, i) in pieces:
                        cols_ref[i, n * tile : (n + 1) * tile] = pieces[d, i][...]

    for i in range(len(near)):
        total = product(high_ref[i], low_ref[i], cols_ref[i])
        for n, (t, s) in enumerate(parts):
            for j in range(len(far)):
                block = total[j * tile : (j + 1) * tile, n * tile : (n + 1) * tile]
                emit(outs[t * len(far) + j], block, (s * len(near) + i) * tile)


def second_kernel(vox, levels, have, far, near, high_ref, low_ref, *refs):
    pieces = dict(zip(have, refs))
    ins, outs = refs[len(have) : -vox * len(far)], refs[-vox * len(far) :]
    for known, out in zip(ins, outs):
        out[...] = known[...]
    tile, slots = refs[0].shape[0], levels // vox
    v, z = lax.axis_index("vox"), lax.axis_index("row")
    for t in range(vox):
        for s in range(slots):
            dist = z - (lax.rem(v + t, vox) * slots + s)
            for (d, i), piece in pieces.items():

                @pl.when(dist == d)
                def _():
                    total = product(high_ref[i], low_ref[i], piece[...])
                    for j in range(len(far)):
                        block = total[j * tile : (j + 1) * tile]
                        emit(outs[t * len(far) + j], block, (s * len(near) + i) * tile)


def multiply(high, low, first, second, levels, vox, far, near):
    tile, depth = first[0, 0].shape
    heights = [tile] + [tile + EXTRA] * (vox * len(far) - 1)
    likes = [jax.ShapeDtypeStruct((h, levels // vox * len(near) * tile), jnp.float32) for h in heights]
    shares = kernel_call(
        functools.partial(first_kernel, vox, levels, list(first), far, near),
        [VMEM] * (2 + len(first)),
        likes,
        [pltpu.VMEM((len(near), levels * tile, depth), jnp.bfloat16)],
    )(high, low, *first.values())
    if second:
        shares = kernel_call(
            functools.partial(second_kernel, vox, levels, list(second), far, near),
            [VMEM] * (2 + len(second) + len(likes)),
            likes,
        )(high, low, *second.values(), *shares)
    return shares


def place_kernel(vox, levels, lines, far, near, *refs):
    blocks, out_ref, held, sems = refs[:-3], refs[-3], refs[-2], refs[-1]
    tile, slots = blocks[0].shape[0], levels // vox
    v, z, w = (lax.axis_index(a) for a in ("vox", "row", "wl"))
    rows = (z * lines + w) * tile + lax.broadcasted_iota(jnp.int32, (tile, tile), 0)
    copies = []
    for j, f in enumerate(far):
        for s in range(slots):
            for i, e in enumerate(near):
                k = (s * len(near) + i) * tile
                total = 0.0
                for t in range(vox):
                    block = blocks[t * len(far) + j]
                    scale = 1.0 if t == j == 0 else jnp.exp2(block[tile : tile + 1, k : k + 1])
                    total += block[:tile, k : k + tile] * scale
                at = pl.multiple_of((s * lines + (w ^ f ^ e)) * tile, tile)
                cols = v * (slots * lines * tile) + at + lax.broadcasted_iota(jnp.int32, (tile, tile), 1)
                n = len(copies)
                held[n] = jnp.where(cols <= rows, total, 0.0)
                copies.append(pltpu.make_async_copy(held.at[n], out_ref.at[:, pl.ds(at, tile)], sems.at[n]))
                copies[-1].start()
    for copy in copies:
        copy.wait()


def place(blocks, vox, levels, lines, far, near):
    tile = blocks[0].shape[0]
    count = levels // vox * lines
    return pl.pallas_call(
        functools.partial(place_kernel, vox, levels, lines, far, near),
        in_specs=[VMEM] * len(blocks),
        out_specs=pl.BlockSpec(memory_space=pl.ANY),
        out_shape=jax.ShapeDtypeStruct((tile, count * tile), jnp.float32),
        scratch_shapes=[pltpu.VMEM((count, tile, tile), jnp.float32), pltpu.SemaphoreType.DMA((count,))],
        compiler_params=pltpu.CompilerParams(vmem_limit_bytes=LIMIT),
    )(*blocks)


def on_device(jac, extinction, prior_var):
    vox, levels, lines = (lax.axis_size(a) for a in ("vox", "row", "wl"))
    slots = levels // vox
    far = [0, lines // 2] if lines > 1 else [0]
    near = list(range(max(lines // 2, 1)))

    below = {0: jac}
    if levels > 1:
        below[1] = shift(jac, "row", 1)
    others = [swap(jac, "wl", f) for f in far[1:]]
    if levels > 2:
        below[levels - 1] = climb(jac, levels - 1, levels - 1, 1)
    weights, own = prepare(extinction.T, prior_var, jac, far, near)
    if levels > 1:
        below[1], weights, own = lax.optimization_barrier([below[1], weights, own])
    for d in range(2, levels - 1):
        below[d] = climb(below[d - 1], 1, d, levels - d)
    high, low = weigh(weights, [own] + others, far, near)
    below[0] = own
    for d in range(2, levels - 1):
        below[d], high, low = lax.optimization_barrier([below[d], high, low])
    pieces = {(d, 0): x for d, x in below.items()}
    pieces.update({(d, i): swap(x, "wl", e) for d, x in below.items() for i, e in enumerate(near) if i})

    second = {k: x for k, x in pieces.items() if k[0] == levels - 2 > 1 and k[1]}
    first = {k: x for k, x in pieces.items() if k not in second}
    shares = list(multiply(high, low, first, second, levels, vox, far, near))
    for k in range(1, len(shares)):
        t, j = divmod(k, len(far))
        shares[k] = send(shares[k].astype(jnp.float16), t, far[j]).astype(jnp.float32)
    return place(shares, vox, levels, lines, far, near)


def solution(mesh):
    return jax.shard_map(
        on_device,
        mesh=mesh,
        in_specs=(P(("row", "wl"), "vox"), P(), P(None, "vox")),
        out_specs=P(("row", "wl"), "vox"),
        check_vma=False,
    )
```

```python
import functools

import jax
import jax.numpy as jnp
from jax import lax
from jax.experimental import pallas as pl
from jax.experimental.pallas import tpu as pltpu
from jax.sharding import PartitionSpec as P

LIMIT = 16 * 2**20
EXTRA = 16
SMEM = pl.BlockSpec(memory_space=pltpu.SMEM)
VMEM = pl.BlockSpec(memory_space=pltpu.VMEM)


def shift(x, axis, by):
    size = lax.axis_size(axis)
    return lax.ppermute(x, axis, [(i, (i + by) % size) for i in range(size)])


def climb(x, by, lowest, count):
    return lax.ppermute(x, "row", [(i - by, i) for i in range(lowest, lowest + count)])


def swap(x, axis, bit):
    size = lax.axis_size(axis)
    return lax.ppermute(x, axis, [(i, i ^ bit) for i in range(size)])


def send(x, by, bit):
    vox, lines = lax.axis_size("vox"), lax.axis_size("wl")
    pairs = [
        (v * lines + w, (v + by) % vox * lines + (w ^ bit)) for v in range(vox) for w in range(lines)
    ]
    return lax.ppermute(x, ("vox", "wl"), pairs)


def kernel_call(kernel, ins, outs, scratch=()):
    return functools.partial(
        pl.pallas_call,
        kernel,
        in_specs=ins,
        out_specs=[VMEM] * len(outs),
        out_shape=outs,
        scratch_shapes=scratch,
        compiler_params=pltpu.CompilerParams(vmem_limit_bytes=LIMIT),
    )()


def ready(dist, levels):
    return jnp.where(dist <= 1, dist, jnp.where(dist == levels - 1, 2, dist + 1))


def choose(vox, level, phase, slots, levels):
    dists = [jnp.maximum(level - (vox * slots + s), 0) for s in range(slots)]
    keys = [ready(d, levels) for d in dists]
    slot = dist = jnp.int32(0)
    for s in range(slots):
        rank = jnp.int32(0)
        for o in range(slots):
            if o != s:
                first = keys[o] <= keys[s] if o < s else keys[o] < keys[s]
                rank += first.astype(jnp.int32)
        slot = jnp.where(rank == phase, s, slot)
        dist = jnp.where(rank == phase, dists[s], dist)
    return slot, dist


def used(phase, slots, levels):
    out = set()
    rank = lambda d: d if d <= 1 else 2 if d == levels - 1 else d + 1
    for v in range(levels // slots):
        for z in range(levels):
            ds = [max(z - (v * slots + s), 0) for s in range(slots)]
            out.add(sorted(ds, key=rank)[phase])
    return sorted(out)


def prepare_kernel(far, near, extinction_ref, prior_ref, jac_ref, weights_ref, own_ref):
    chroms, waves = extinction_ref.shape
    w = lax.axis_index("wl")
    for i, e in enumerate(near):
        for j, f in enumerate(far):
            weight = 0.0
            for c in range(chroms):
                coeff = extinction_ref[c, lax.rem(w ^ f, waves)] * extinction_ref[c, lax.rem(w ^ e, waves)]
                weight += coeff * prior_ref[c : c + 1, :]
            weights_ref[i * len(far) + j : i * len(far) + j + 1, :] = weight
    own_ref[...] = jac_ref[...]


def prepare(extinction, prior, jac, far, near):
    weights = jax.ShapeDtypeStruct((len(far) * len(near), jac.shape[1]), jnp.float32)
    own = jax.ShapeDtypeStruct(jac.shape, jac.dtype)
    call = kernel_call(functools.partial(prepare_kernel, far, near), [SMEM, VMEM, VMEM], [weights, own])
    return call(extinction, prior, jac)


def weigh_kernel(far, near, weights_ref, *refs):
    rows, (high_ref, low_ref) = refs[:-2], refs[-2:]
    tile = rows[0].shape[0]
    for i in range(len(near)):
        for j in range(len(far)):
            k = i * len(far) + j
            scaled = rows[j][...].astype(jnp.float32) * weights_ref[k : k + 1, :]
            top = scaled.astype(jnp.bfloat16)
            high_ref[i, j * tile : (j + 1) * tile, :] = top
            low_ref[i, j * tile : (j + 1) * tile, :] = (scaled - top.astype(jnp.float32)).astype(jnp.bfloat16)


def weigh(weights, rows, far, near):
    tile, depth = rows[0].shape
    like = jax.ShapeDtypeStruct((len(near), len(far) * tile, depth), jnp.bfloat16)
    call = kernel_call(functools.partial(weigh_kernel, far, near), [VMEM] * (1 + len(rows)), [like, like])
    return call(weights, *rows)


def multiply_kernel(vox, levels, phases, dists, far, near, high_ref, low_ref, *refs):
    count = len(dists) * len(near)
    pieces, outs, cols_ref = refs[:count], refs[count:-1], refs[-1]
    tile = pieces[0].shape[0]
    v, z = lax.axis_index("vox"), lax.axis_index("row")
    parts = [(t, p) for t in range(vox) for p in range(len(phases))]
    for n, (t, p) in enumerate(parts):
        _, dist = choose(lax.rem(v + t, vox), z, phases[p], levels // vox, levels)
        for k, d in enumerate(dists):

            @pl.when(dist == d)
            def _():
                for i in range(len(near)):
                    cols_ref[i, n * tile : (n + 1) * tile] = pieces[k * len(near) + i][...]

    slots = levels // vox
    owners = [choose(o, z, p, slots, levels)[0] + o * slots for o in range(vox) for p in phases]
    needed = functools.reduce(jnp.logical_or, [at <= z for at in owners])

    @pl.when(jnp.logical_not(needed))
    def _():
        for out in outs:
            out[...] = jnp.zeros_like(out)

    @pl.when(needed)
    def _():
        for i in range(len(near)):
            total = 0.0
            for part in (high_ref, low_ref):
                total += lax.dot_general(
                    part[i], cols_ref[i], (((1,), (1,)), ((), ())), preferred_element_type=jnp.float32
                )
            for n, (t, p) in enumerate(parts):
                to = (p * len(near) + i) * tile
                for j in range(len(far)):
                    outs[t * len(far) + j][:tile, to : to + tile] = total[
                        j * tile : (j + 1) * tile, n * tile : (n + 1) * tile
                    ]
        for out in outs[1:]:
            largest = jnp.max(jnp.abs(out[:tile]), axis=(0, 1), keepdims=True)
            power = jnp.floor(jnp.log2(jnp.maximum(largest, 1e-30))) - 13.0
            out[:tile] *= jnp.exp2(-power)
            out[tile:] = jnp.broadcast_to(power, out[tile:].shape)


def multiply(high, low, pieces, levels, vox, phases, far, near):
    tile, depth = pieces[0][0].shape
    dists = sorted(set().union(*[used(p, levels // vox, levels) for p in phases]))
    flat = [pieces[d][i] for d in dists for i in range(len(near))]
    heights = [tile] + [tile + EXTRA] * (vox * len(far) - 1)
    width = len(phases) * len(near) * tile
    call = kernel_call(
        functools.partial(multiply_kernel, vox, levels, phases, dists, far, near),
        [VMEM] * (2 + len(flat)),
        [jax.ShapeDtypeStruct((height, width), jnp.float32) for height in heights],
        [pltpu.VMEM((len(near), vox * len(phases) * tile, depth), jnp.bfloat16)],
    )
    return call(high, low, *flat)


def place_kernel(vox, levels, lines, groups, far, near, *refs):
    blocks, out_ref = refs[-2::-1], refs[-1]
    tile, slots = out_ref.shape[0], levels // vox
    v, z, w = (lax.axis_index(a) for a in ("vox", "row", "wl"))
    rows = (z * lines + w) * tile + lax.broadcasted_iota(jnp.int32, (tile, tile), 0)
    for g, phases in enumerate(groups):
        for p, phase in enumerate(phases):
            slot, _ = choose(v, z, phase, slots, levels)
            for j, f in enumerate(far):
                for i, e in enumerate(near):
                    src = slice((p * len(near) + i) * tile, (p * len(near) + i + 1) * tile)
                    total = 0.0
                    for t in range(vox):
                        block = blocks[(g * vox + t) * len(far) + j]
                        scale = 1.0 if t == j == 0 else jnp.exp2(block[tile : tile + 1, :1])
                        total += block[:tile, src] * scale
                    at = pl.multiple_of((slot * lines + (w ^ f ^ e)) * tile, tile)
                    cols = v * (slots * lines * tile) + at + lax.broadcasted_iota(jnp.int32, (tile, tile), 1)
                    out_ref[:, pl.ds(at, tile)] = jnp.where(cols <= rows, total, 0.0)


def place(blocks, vox, levels, lines, groups, far, near):
    tile = blocks[0].shape[0]
    call = kernel_call(
        functools.partial(place_kernel, vox, levels, lines, groups, far, near),
        [VMEM] * len(blocks),
        [jax.ShapeDtypeStruct((tile, levels // vox * lines * tile), jnp.float32)],
    )
    return call(*blocks[::-1])[0]


def on_device(jac, extinction, prior_var):
    vox, levels, lines = (lax.axis_size(a) for a in ("vox", "row", "wl"))
    tile, slots = jac.shape[0], levels // vox
    far = [0, lines // 2] if lines > 1 else [0]
    near = list(range(max(lines // 2, 1)))

    groups = [[p] for p in range(slots)]

    below = {0: jac}
    if levels > 1:
        below[1] = shift(jac, "row", 1)
    others = [swap(jac, "wl", f) for f in far[1:]]
    if levels > 2:
        below[levels - 1] = climb(jac, levels - 1, levels - 1, 1)
    weights, own = prepare(extinction.T, prior_var, jac, far, near)
    if levels > 1:
        below[1], weights, own = lax.optimization_barrier([below[1], weights, own])
    for d in range(2, levels - 1):
        below[d] = climb(below[d - 1], 1, d, levels - d)
    high, low = weigh(weights, [own] + others, far, near)
    below[0] = own

    def both(d):
        cuts = (below[d],) if d == 0 else (below[d][: tile // 2], below[d][tile // 2 :])
        swapped = [[swap(x, "wl", e) for x in cuts] for e in near[1:]]
        return [below[d]] + [jnp.concatenate(xs, axis=0) if d else xs[0] for xs in swapped]

    pieces = {d: both(d) for d in (0, 1, levels - 1)}
    blocks = []
    for phases in groups:
        dists = sorted(set().union(*[used(p, slots, levels) for p in phases]))
        late = [d for d in dists if d not in pieces]
        if late:
            flat = lax.optimization_barrier([below[d] for d in late] + blocks)
            blocks = list(flat[len(late) :])
            for d, x in zip(late, flat):
                pieces[d] = [x] + [swap(x, "wl", e) for e in near[1:]]
        shares = multiply(high, low, pieces, levels, vox, phases, far, near)
        blocks += [share.astype(jnp.float16) if k else share for k, share in enumerate(shares)]
    sent = []
    for k, share in enumerate(blocks):
        t, j = divmod(k % (vox * len(far)), len(far))
        sent.append(send(share, t, far[j]).astype(jnp.float32) if t or j else share)
    return place(sent, vox, levels, lines, groups, far, near)


def solution(mesh):
    return jax.shard_map(
        on_device,
        mesh=mesh,
        in_specs=(P(("row", "wl"), "vox"), P(), P(None, "vox")),
        out_specs=P(("row", "wl"), "vox"),
        check_vma=False,
    )
```

```python
import functools

import jax
import jax.numpy as jnp
from jax import lax
from jax.experimental import pallas as pl
from jax.experimental.pallas import tpu as pltpu
from jax.sharding import PartitionSpec as P

LIMIT = 16 * 2**20
EXTRA = 16
SMEM = pl.BlockSpec(memory_space=pltpu.SMEM)
VMEM = pl.BlockSpec(memory_space=pltpu.VMEM)


def shift(x, axis, by):
    size = lax.axis_size(axis)
    return lax.ppermute(x, axis, [(i, (i + by) % size) for i in range(size)])


def climb(x, by, lowest, count):
    return lax.ppermute(x, "row", [(i - by, i) for i in range(lowest, lowest + count)])


def swap(x, axis, bit):
    size = lax.axis_size(axis)
    return lax.ppermute(x, axis, [(i, i ^ bit) for i in range(size)])


def send(x, by, bit):
    vox, lines = lax.axis_size("vox"), lax.axis_size("wl")
    pairs = [
        (v * lines + w, (v + by) % vox * lines + (w ^ bit)) for v in range(vox) for w in range(lines)
    ]
    return lax.ppermute(x, ("vox", "wl"), pairs)


def kernel_call(kernel, ins, outs, scratch=(), cost=None):
    return functools.partial(
        pl.pallas_call,
        kernel,
        in_specs=ins,
        out_specs=[VMEM] * len(outs),
        out_shape=outs,
        scratch_shapes=scratch,
        compiler_params=pltpu.CompilerParams(vmem_limit_bytes=LIMIT),
        cost_estimate=cost,
    )()


def ready(dist, levels):
    return jnp.where(dist <= 1, dist, jnp.where(dist == levels - 1, 2, dist + 1))


def choose(vox, level, phase, slots, levels):
    dists = [jnp.maximum(level - (vox * slots + s), 0) for s in range(slots)]
    keys = [ready(d, levels) for d in dists]
    slot = dist = jnp.int32(0)
    for s in range(slots):
        rank = jnp.int32(0)
        for o in range(slots):
            if o != s:
                first = keys[o] <= keys[s] if o < s else keys[o] < keys[s]
                rank += first.astype(jnp.int32)
        slot = jnp.where(rank == phase, s, slot)
        dist = jnp.where(rank == phase, dists[s], dist)
    return slot, dist


def used(phase, slots, levels):
    out = set()
    rank = lambda d: d if d <= 1 else 2 if d == levels - 1 else d + 1
    for v in range(levels // slots):
        for z in range(levels):
            ds = [max(z - (v * slots + s), 0) for s in range(slots)]
            out.add(sorted(ds, key=rank)[phase])
    return sorted(out)


def prepare_kernel(far, near, extinction_ref, prior_ref, jac_ref, weights_ref, own_ref):
    chroms, waves = extinction_ref.shape
    w = lax.axis_index("wl")
    for i, e in enumerate(near):
        for j, f in enumerate(far):
            weight = 0.0
            for c in range(chroms):
                coeff = extinction_ref[c, lax.rem(w ^ f, waves)] * extinction_ref[c, lax.rem(w ^ e, waves)]
                weight += coeff * prior_ref[c : c + 1, :]
            weights_ref[i * len(far) + j : i * len(far) + j + 1, :] = weight
    own_ref[...] = jac_ref[...]


def prepare(extinction, prior, jac, far, near):
    weights = jax.ShapeDtypeStruct((len(far) * len(near), jac.shape[1]), jnp.float32)
    own = jax.ShapeDtypeStruct(jac.shape, jac.dtype)
    call = kernel_call(functools.partial(prepare_kernel, far, near), [SMEM, VMEM, VMEM], [weights, own], cost=pl.CostEstimate(flops=1, bytes_accessed=8000000, transcendentals=0))
    return call(extinction, prior, jac)


def weigh_kernel(far, near, weights_ref, *refs):
    rows, (high_ref, low_ref) = refs[:-2], refs[-2:]
    tile = rows[0].shape[0]
    for i in range(len(near)):
        for j in range(len(far)):
            k = i * len(far) + j
            scaled = rows[j][...].astype(jnp.float32) * weights_ref[k : k + 1, :]
            top = scaled.astype(jnp.bfloat16)
            high_ref[i, j * tile : (j + 1) * tile, :] = top
            low_ref[i, j * tile : (j + 1) * tile, :] = (scaled - top.astype(jnp.float32)).astype(jnp.bfloat16)


def weigh(weights, rows, far, near):
    tile, depth = rows[0].shape
    like = jax.ShapeDtypeStruct((len(near), len(far) * tile, depth), jnp.bfloat16)
    call = kernel_call(functools.partial(weigh_kernel, far, near), [VMEM] * (1 + len(rows)), [like, like], cost=pl.CostEstimate(flops=1, bytes_accessed=1, transcendentals=0))
    return call(weights, *rows)


def multiply_kernel(vox, levels, phases, dists, far, near, high_ref, low_ref, *refs):
    count = len(dists) * len(near)
    pieces, outs, cols_ref = refs[:count], refs[count:-1], refs[-1]
    tile = pieces[0].shape[0]
    v, z = lax.axis_index("vox"), lax.axis_index("row")
    parts = [(t, p) for t in range(vox) for p in range(len(phases))]
    for n, (t, p) in enumerate(parts):
        _, dist = choose(lax.rem(v + t, vox), z, phases[p], levels // vox, levels)
        for k, d in enumerate(dists):

            @pl.when(dist == d)
            def _():
                for i in range(len(near)):
                    cols_ref[i, n * tile : (n + 1) * tile] = pieces[k * len(near) + i][...]

    slots = levels // vox
    owners = [choose(o, z, p, slots, levels)[0] + o * slots for o in range(vox) for p in phases]
    needed = functools.reduce(jnp.logical_or, [at <= z for at in owners])

    @pl.when(jnp.logical_not(needed))
    def _():
        for out in outs:
            out[...] = jnp.zeros_like(out)

    @pl.when(needed)
    def _():
        for i in range(len(near)):
            total = 0.0
            for part in (high_ref, low_ref):
                total += lax.dot_general(
                    part[i], cols_ref[i], (((1,), (1,)), ((), ())), preferred_element_type=jnp.float32
                )
            for n, (t, p) in enumerate(parts):
                to = (p * len(near) + i) * tile
                for j in range(len(far)):
                    outs[t * len(far) + j][:tile, to : to + tile] = total[
                        j * tile : (j + 1) * tile, n * tile : (n + 1) * tile
                    ]
        for out in outs[1:]:
            largest = jnp.max(jnp.abs(out[:tile]), axis=(0, 1), keepdims=True)
            power = jnp.floor(jnp.log2(jnp.maximum(largest, 1e-30))) - 13.0
            out[:tile] *= jnp.exp2(-power)
            out[tile:] = jnp.broadcast_to(power, out[tile:].shape)


def multiply(high, low, pieces, levels, vox, phases, far, near):
    tile, depth = pieces[0][0].shape
    dists = sorted(set().union(*[used(p, levels // vox, levels) for p in phases]))
    flat = [pieces[d][i] for d in dists for i in range(len(near))]
    heights = [tile] + [tile + EXTRA] * (vox * len(far) - 1)
    width = len(phases) * len(near) * tile
    call = kernel_call(
        functools.partial(multiply_kernel, vox, levels, phases, dists, far, near),
        [VMEM] * (2 + len(flat)),
        [jax.ShapeDtypeStruct((height, width), jnp.float32) for height in heights],
        [pltpu.VMEM((len(near), vox * len(phases) * tile, depth), jnp.bfloat16)],
        None if phases[0] == 0 else None,
    )
    return call(high, low, *flat)


def place_kernel(vox, levels, lines, groups, far, near, *refs):
    perm = [7, 6, 5, 4, 3, 1, 2, 0] if len(refs) == 9 else range(len(refs) - 1)
    blocks, out_ref = [refs[list(perm).index(k)] for k in range(len(refs) - 1)], refs[-1]
    tile, slots = out_ref.shape[0], levels // vox
    v, z, w = (lax.axis_index(a) for a in ("vox", "row", "wl"))
    rows = (z * lines + w) * tile + lax.broadcasted_iota(jnp.int32, (tile, tile), 0)
    for g, phases in enumerate(groups):
        for p, phase in enumerate(phases):
            slot, _ = choose(v, z, phase, slots, levels)
            for j, f in enumerate(far):
                for i, e in enumerate(near):
                    src = slice((p * len(near) + i) * tile, (p * len(near) + i + 1) * tile)
                    total = 0.0
                    for t in range(vox):
                        block = blocks[(g * vox + t) * len(far) + j]
                        scale = 1.0 if t == j == 0 else jnp.exp2(block[tile : tile + 1, :1])
                        total += block[:tile, src] * scale
                    at = pl.multiple_of((slot * lines + (w ^ f ^ e)) * tile, tile)
                    cols = v * (slots * lines * tile) + at + lax.broadcasted_iota(jnp.int32, (tile, tile), 1)
                    out_ref[:, pl.ds(at, tile)] = jnp.where(cols <= rows, total, 0.0)


def place(blocks, vox, levels, lines, groups, far, near):
    tile = blocks[0].shape[0]
    call = kernel_call(
        functools.partial(place_kernel, vox, levels, lines, groups, far, near),
        [VMEM] * len(blocks),
        [jax.ShapeDtypeStruct((tile, levels // vox * lines * tile), jnp.float32)],
    )
    perm = [7, 6, 5, 4, 3, 1, 2, 0] if len(blocks) == 8 else range(len(blocks))
    return call(*[blocks[k] for k in perm])[0]


def on_device(jac, extinction, prior_var):
    vox, levels, lines = (lax.axis_size(a) for a in ("vox", "row", "wl"))
    tile, slots = jac.shape[0], levels // vox
    far = [0, lines // 2] if lines > 1 else [0]
    near = list(range(max(lines // 2, 1)))

    groups = [[p] for p in range(slots)]

    below = {0: jac}
    if levels > 1:
        below[1] = shift(jac, "row", 1)
    others = [swap(jac, "wl", f) for f in far[1:]]
    if levels > 2:
        below[levels - 1] = climb(jac, levels - 1, levels - 1, 1)
    weights, own = prepare(extinction.T, prior_var, jac, far, near)
    if levels > 1:
        below[1], weights, own = lax.optimization_barrier([below[1], weights, own])
    for d in range(2, levels - 1):
        below[d] = climb(below[d - 1], 1, d, levels - d)
    high, low = weigh(weights, [own] + others, far, near)
    below[0] = own

    def both(d):
        n = {0: 1, 1: 2}.get(d, 2)
        cuts = [below[d][k * tile // n : (k + 1) * tile // n] for k in range(n)]
        swapped = [[swap(x, "wl", e) for x in cuts] for e in near[1:]]
        return [below[d]] + [jnp.concatenate(xs, axis=0) if len(xs) > 1 else xs[0] for xs in swapped]

    pieces = {d: both(d) for d in (0, 1, levels - 1)}
    blocks = []
    for phases in groups:
        dists = sorted(set().union(*[used(p, slots, levels) for p in phases]))
        late = [d for d in dists if d not in pieces]
        if late:
            flat = lax.optimization_barrier([below[d] for d in late] + blocks)
            blocks = list(flat[len(late) :])
            for d, x in zip(late, flat):
                pieces[d] = [x] + [swap(x, "wl", e) for e in near[1:]]
        shares = multiply(high, low, pieces, levels, vox, phases, far, near)
        blocks += [share.astype(jnp.float16) if k else share for k, share in enumerate(shares)]
    sent = []
    for k, share in enumerate(blocks):
        t, j = divmod(k % (vox * len(far)), len(far))
        sent.append(send(share, t, far[j]).astype(jnp.float32) if t or j else share)
    return place(sent, vox, levels, lines, groups, far, near)


def solution(mesh):
    return jax.shard_map(
        on_device,
        mesh=mesh,
        in_specs=(P(("row", "wl"), "vox"), P(), P(None, "vox")),
        out_specs=P(("row", "wl"), "vox"),
        check_vma=False,
    )
```

```python
import functools

import jax
import jax.numpy as jnp
from jax import lax
from jax.experimental import pallas as pl
from jax.experimental.pallas import tpu as pltpu
from jax.sharding import PartitionSpec as P

LIMIT = 16 * 2**20
EXTRA = 16
SMEM = pl.BlockSpec(memory_space=pltpu.SMEM)
VMEM = pl.BlockSpec(memory_space=pltpu.VMEM)


def shift(x, axis, by):
    size = lax.axis_size(axis)
    return lax.ppermute(x, axis, [(i, (i + by) % size) for i in range(size)])


def climb(x, by, lowest, count):
    return lax.ppermute(x, "row", [(i - by, i) for i in range(lowest, lowest + count)])


def swap(x, axis, bit):
    size = lax.axis_size(axis)
    return lax.ppermute(x, axis, [(i, i ^ bit) for i in range(size)])


def send(x, by, bit):
    vox, lines = lax.axis_size("vox"), lax.axis_size("wl")
    pairs = [
        (v * lines + w, (v + by) % vox * lines + (w ^ bit)) for v in range(vox) for w in range(lines)
    ]
    return lax.ppermute(x, ("vox", "wl"), pairs)


def kernel_call(kernel, ins, outs, scratch=(), cost=None):
    return functools.partial(
        pl.pallas_call,
        kernel,
        in_specs=ins,
        out_specs=[VMEM] * len(outs),
        out_shape=outs,
        scratch_shapes=scratch,
        compiler_params=pltpu.CompilerParams(vmem_limit_bytes=LIMIT),
        cost_estimate=cost,
    )()


def ready(dist, levels):
    return jnp.where(dist <= 1, dist, jnp.where(dist == levels - 1, 2, dist + 1))


def choose(vox, level, phase, slots, levels):
    dists = [jnp.maximum(level - (vox * slots + s), 0) for s in range(slots)]
    keys = [ready(d, levels) for d in dists]
    slot = dist = jnp.int32(0)
    for s in range(slots):
        rank = jnp.int32(0)
        for o in range(slots):
            if o != s:
                first = keys[o] <= keys[s] if o < s else keys[o] < keys[s]
                rank += first.astype(jnp.int32)
        slot = jnp.where(rank == phase, s, slot)
        dist = jnp.where(rank == phase, dists[s], dist)
    return slot, dist


def used(phase, slots, levels):
    out = set()
    rank = lambda d: d if d <= 1 else 2 if d == levels - 1 else d + 1
    for v in range(levels // slots):
        for z in range(levels):
            ds = [max(z - (v * slots + s), 0) for s in range(slots)]
            out.add(sorted(ds, key=rank)[phase])
    return sorted(out)


def prepare_kernel(far, near, extinction_ref, prior_ref, jac_ref, weights_ref, own_ref):
    chroms, waves = extinction_ref.shape
    w = lax.axis_index("wl")
    for i, e in enumerate(near):
        for j, f in enumerate(far):
            weight = 0.0
            for c in range(chroms):
                coeff = extinction_ref[c, lax.rem(w ^ f, waves)] * extinction_ref[c, lax.rem(w ^ e, waves)]
                weight += coeff * prior_ref[c : c + 1, :]
            weights_ref[i * len(far) + j : i * len(far) + j + 1, :] = weight
    own_ref[...] = jac_ref[...]


def prepare(extinction, prior, jac, far, near):
    weights = jax.ShapeDtypeStruct((len(far) * len(near), jac.shape[1]), jnp.float32)
    own = jax.ShapeDtypeStruct(jac.shape, jac.dtype)
    call = kernel_call(functools.partial(prepare_kernel, far, near), [SMEM, VMEM, VMEM], [weights, own], cost=pl.CostEstimate(flops=1, bytes_accessed=8000000, transcendentals=0))
    return call(extinction, prior, jac)


def weigh_kernel(far, near, weights_ref, *refs):
    rows, (high_ref, low_ref) = refs[:-2], refs[-2:]
    tile = rows[0].shape[0]
    for i in range(len(near)):
        for j in range(len(far)):
            k = i * len(far) + j
            scaled = rows[j][...].astype(jnp.float32) * weights_ref[k : k + 1, :]
            top = scaled.astype(jnp.bfloat16)
            high_ref[i, j * tile : (j + 1) * tile, :] = top
            low_ref[i, j * tile : (j + 1) * tile, :] = (scaled - top.astype(jnp.float32)).astype(jnp.bfloat16)


def weigh(weights, rows, far, near):
    tile, depth = rows[0].shape
    like = jax.ShapeDtypeStruct((len(near), len(far) * tile, depth), jnp.bfloat16)
    call = kernel_call(functools.partial(weigh_kernel, far, near), [VMEM] * (1 + len(rows)), [like, like], cost=pl.CostEstimate(flops=1, bytes_accessed=1, transcendentals=0))
    return call(weights, *rows)


def multiply_kernel(vox, levels, phases, dists, far, near, high_ref, low_ref, *refs):
    count = len(dists) * len(near)
    pieces, outs, cols_ref = refs[:count], refs[count:-1], refs[-1]
    tile = pieces[0].shape[0]
    v, z = lax.axis_index("vox"), lax.axis_index("row")
    parts = [(t, p) for t in range(vox) for p in range(len(phases))]
    for n, (t, p) in enumerate(parts):
        _, dist = choose(lax.rem(v + t, vox), z, phases[p], levels // vox, levels)
        for k, d in enumerate(dists):

            @pl.when(dist == d)
            def _():
                for i in range(len(near)):
                    cols_ref[i, n * tile : (n + 1) * tile] = pieces[k * len(near) + i][...]

    slots = levels // vox
    owners = [choose(o, z, p, slots, levels)[0] + o * slots for o in range(vox) for p in phases]
    needed = functools.reduce(jnp.logical_or, [at <= z for at in owners])

    @pl.when(jnp.logical_not(needed))
    def _():
        for out in outs:
            out[...] = jnp.zeros_like(out)

    @pl.when(needed)
    def _():
        for i in range(len(near)):
            total = 0.0
            for part in (high_ref, low_ref):
                total += lax.dot_general(
                    part[i], cols_ref[i], (((1,), (1,)), ((), ())), preferred_element_type=jnp.float32
                )
            for n, (t, p) in enumerate(parts):
                to = (p * len(near) + i) * tile
                for j in range(len(far)):
                    outs[t * len(far) + j][:tile, to : to + tile] = total[
                        j * tile : (j + 1) * tile, n * tile : (n + 1) * tile
                    ]
        for out in outs[1:]:
            largest = jnp.max(jnp.abs(out[:tile]), axis=(0, 1), keepdims=True)
            power = jnp.floor(jnp.log2(jnp.maximum(largest, 1e-30))) - 13.0
            out[:tile] *= jnp.exp2(-power)
            out[tile:] = jnp.broadcast_to(power, out[tile:].shape)


def multiply(high, low, pieces, levels, vox, phases, far, near):
    tile, depth = pieces[0][0].shape
    dists = sorted(set().union(*[used(p, levels // vox, levels) for p in phases]))
    flat = [pieces[d][i] for d in dists for i in range(len(near))]
    heights = [tile] + [tile + EXTRA] * (vox * len(far) - 1)
    width = len(phases) * len(near) * tile
    call = kernel_call(
        functools.partial(multiply_kernel, vox, levels, phases, dists, far, near),
        [VMEM] * (2 + len(flat)),
        [jax.ShapeDtypeStruct((height, width), jnp.float32) for height in heights],
        [pltpu.VMEM((len(near), vox * len(phases) * tile, depth), jnp.bfloat16)],
        None if phases[0] == 0 else None,
    )
    return call(high, low, *flat)


def place_kernel(vox, levels, lines, groups, far, near, *refs):
    perm = [7, 6, 5, 4, 3, 1, 2, 0] if len(refs) == 11 else range(len(refs) - 3)
    blocks, (out_ref, held, sems) = [refs[list(perm).index(k)] for k in range(len(refs) - 3)], refs[-3:]
    copies = []
    tile, slots = out_ref.shape[0], levels // vox
    v, z, w = (lax.axis_index(a) for a in ("vox", "row", "wl"))
    rows = (z * lines + w) * tile + lax.broadcasted_iota(jnp.int32, (tile, tile), 0)
    for g, phases in enumerate(groups):
        for p, phase in enumerate(phases):
            slot, _ = choose(v, z, phase, slots, levels)
            for j, f in enumerate(far):
                for i, e in enumerate(near):
                    src = slice((p * len(near) + i) * tile, (p * len(near) + i + 1) * tile)
                    total = 0.0
                    for t in range(vox):
                        block = blocks[(g * vox + t) * len(far) + j]
                        scale = 1.0 if t == j == 0 else jnp.exp2(block[tile : tile + 1, :1])
                        total += block[:tile, src] * scale
                    at = pl.multiple_of((slot * lines + (w ^ f ^ e)) * tile, tile)
                    cols = v * (slots * lines * tile) + at + lax.broadcasted_iota(jnp.int32, (tile, tile), 1)
                    n = len(copies)
                    held[n] = jnp.where(cols <= rows, total, 0.0)
                    copies.append(pltpu.make_async_copy(held.at[n], out_ref.at[:, pl.ds(at, tile)], sems.at[n]))
                    copies[-1].start()
    for copy in copies:
        copy.wait()


def place(blocks, vox, levels, lines, groups, far, near):
    tile = blocks[0].shape[0]
    count = levels // vox * lines
    perm = [7, 6, 5, 4, 3, 1, 2, 0] if len(blocks) == 8 else range(len(blocks))
    return pl.pallas_call(
        functools.partial(place_kernel, vox, levels, lines, groups, far, near),
        in_specs=[VMEM] * len(blocks),
        out_specs=pl.BlockSpec(memory_space=pl.ANY),
        out_shape=jax.ShapeDtypeStruct((tile, count * tile), jnp.float32),
        scratch_shapes=[pltpu.VMEM((count, tile, tile), jnp.float32), pltpu.SemaphoreType.DMA((count,))],
        compiler_params=pltpu.CompilerParams(vmem_limit_bytes=LIMIT),
    )(*[blocks[k] for k in perm])


def on_device(jac, extinction, prior_var):
    vox, levels, lines = (lax.axis_size(a) for a in ("vox", "row", "wl"))
    tile, slots = jac.shape[0], levels // vox
    far = [0, lines // 2] if lines > 1 else [0]
    near = list(range(max(lines // 2, 1)))

    groups = [[p] for p in range(slots)]

    below = {0: jac}
    if levels > 1:
        below[1] = shift(jac, "row", 1)
    others = [swap(jac, "wl", f) for f in far[1:]]
    if levels > 2:
        below[levels - 1] = climb(jac, levels - 1, levels - 1, 1)
    weights, own = prepare(extinction.T, prior_var, jac, far, near)
    if levels > 1:
        below[1], weights, own = lax.optimization_barrier([below[1], weights, own])
    for d in range(2, levels - 1):
        below[d] = climb(below[d - 1], 1, d, levels - d)
    high, low = weigh(weights, [own] + others, far, near)
    below[0] = own

    def both(d):
        n = {0: 1, 1: 2}.get(d, 2)
        cuts = [below[d][k * tile // n : (k + 1) * tile // n] for k in range(n)]
        swapped = [[swap(x, "wl", e) for x in cuts] for e in near[1:]]
        return [below[d]] + [jnp.concatenate(xs, axis=0) if len(xs) > 1 else xs[0] for xs in swapped]

    pieces = {d: both(d) for d in (0, 1, levels - 1)}
    blocks = []
    for phases in groups:
        dists = sorted(set().union(*[used(p, slots, levels) for p in phases]))
        late = [d for d in dists if d not in pieces]
        if late:
            flat = lax.optimization_barrier([below[d] for d in late] + blocks)
            blocks = list(flat[len(late) :])
            for d, x in zip(late, flat):
                pieces[d] = [x] + [swap(x, "wl", e) for e in near[1:]]
        shares = multiply(high, low, pieces, levels, vox, phases, far, near)
        blocks += [share.astype(jnp.float16) if k else share for k, share in enumerate(shares)]
    sent = []
    for k, share in enumerate(blocks):
        t, j = divmod(k % (vox * len(far)), len(far))
        sent.append(send(share, t, far[j]).astype(jnp.float32) if t or j else share)
    return place(sent, vox, levels, lines, groups, far, near)


def solution(mesh):
    return jax.shard_map(
        on_device,
        mesh=mesh,
        in_specs=(P(("row", "wl"), "vox"), P(), P(None, "vox")),
        out_specs=P(("row", "wl"), "vox"),
        check_vma=False,
    )
```

```python
import functools

import jax
import jax.numpy as jnp
from jax import lax
from jax.experimental import pallas as pl
from jax.experimental.pallas import tpu as pltpu
from jax.sharding import PartitionSpec as P

LIMIT = 16 * 2**20
EXTRA = 16
SMEM = pl.BlockSpec(memory_space=pltpu.SMEM)
VMEM = pl.BlockSpec(memory_space=pltpu.VMEM)


def shift(x, axis, by):
    size = lax.axis_size(axis)
    return lax.ppermute(x, axis, [(i, (i + by) % size) for i in range(size)])


def climb(x, by, lowest, count):
    return lax.ppermute(x, "row", [(i - by, i) for i in range(lowest, lowest + count)])


def swap(x, axis, bit):
    size = lax.axis_size(axis)
    return lax.ppermute(x, axis, [(i, i ^ bit) for i in range(size)])


def send(x, by, bit):
    vox, lines = lax.axis_size("vox"), lax.axis_size("wl")
    pairs = [
        (v * lines + w, (v + by) % vox * lines + (w ^ bit)) for v in range(vox) for w in range(lines)
    ]
    return lax.ppermute(x, ("vox", "wl"), pairs)


def kernel_call(kernel, ins, outs, scratch=(), cost=None):
    return functools.partial(
        pl.pallas_call,
        kernel,
        in_specs=ins,
        out_specs=[VMEM] * len(outs),
        out_shape=outs,
        scratch_shapes=scratch,
        compiler_params=pltpu.CompilerParams(vmem_limit_bytes=LIMIT),
        cost_estimate=cost,
    )()


def ready(dist, levels):
    return jnp.where(dist <= 1, dist, jnp.where(dist == levels - 1, 2, dist + 1))


def choose(vox, level, phase, slots, levels):
    dists = [jnp.maximum(level - (vox * slots + s), 0) for s in range(slots)]
    keys = [ready(d, levels) for d in dists]
    slot = dist = jnp.int32(0)
    for s in range(slots):
        rank = jnp.int32(0)
        for o in range(slots):
            if o != s:
                first = keys[o] <= keys[s] if o < s else keys[o] < keys[s]
                rank += first.astype(jnp.int32)
        slot = jnp.where(rank == phase, s, slot)
        dist = jnp.where(rank == phase, dists[s], dist)
    return slot, dist


def used(phase, slots, levels):
    out = set()
    rank = lambda d: d if d <= 1 else 2 if d == levels - 1 else d + 1
    for v in range(levels // slots):
        for z in range(levels):
            ds = [max(z - (v * slots + s), 0) for s in range(slots)]
            out.add(sorted(ds, key=rank)[phase])
    return sorted(out)


def prepare_kernel(far, near, extinction_ref, prior_ref, jac_ref, weights_ref, own_ref):
    chroms, waves = extinction_ref.shape
    w = lax.axis_index("wl")
    for i, e in enumerate(near):
        for j, f in enumerate(far):
            weight = 0.0
            for c in range(chroms):
                coeff = extinction_ref[c, lax.rem(w ^ f, waves)] * extinction_ref[c, lax.rem(w ^ e, waves)]
                weight += coeff * prior_ref[c : c + 1, :]
            weights_ref[i * len(far) + j : i * len(far) + j + 1, :] = weight
    own_ref[...] = jac_ref[...]


def prepare(extinction, prior, jac, far, near):
    weights = jax.ShapeDtypeStruct((len(far) * len(near), jac.shape[1]), jnp.float32)
    own = jax.ShapeDtypeStruct(jac.shape, jac.dtype)
    call = kernel_call(functools.partial(prepare_kernel, far, near), [SMEM, VMEM, VMEM], [weights, own])
    return call(extinction, prior, jac)


def weigh_kernel(far, near, weights_ref, *refs):
    rows, (high_ref, low_ref) = refs[:-2], refs[-2:]
    tile = rows[0].shape[0]
    for i in range(len(near)):
        for j in range(len(far)):
            k = i * len(far) + j
            scaled = rows[j][...].astype(jnp.float32) * weights_ref[k : k + 1, :]
            top = scaled.astype(jnp.bfloat16)
            high_ref[i, j * tile : (j + 1) * tile, :] = top
            low_ref[i, j * tile : (j + 1) * tile, :] = (scaled - top.astype(jnp.float32)).astype(jnp.bfloat16)


def weigh(weights, rows, far, near):
    tile, depth = rows[0].shape
    like = jax.ShapeDtypeStruct((len(near), len(far) * tile, depth), jnp.bfloat16)
    call = kernel_call(functools.partial(weigh_kernel, far, near), [VMEM] * (1 + len(rows)), [like, like])
    return call(weights, *rows)


def multiply_kernel(vox, levels, phases, dists, far, near, high_ref, low_ref, *refs):
    count = len(dists) * len(near)
    pieces, outs, cols_ref = refs[:count], refs[count:-1], refs[-1]
    tile = pieces[0].shape[0]
    v, z = lax.axis_index("vox"), lax.axis_index("row")
    parts = [(t, p) for t in range(vox) for p in range(len(phases))]
    for n, (t, p) in enumerate(parts):
        _, dist = choose(lax.rem(v + t, vox), z, phases[p], levels // vox, levels)
        for k, d in enumerate(dists):

            @pl.when(dist == d)
            def _():
                for i in range(len(near)):
                    cols_ref[i, n * tile : (n + 1) * tile] = pieces[k * len(near) + i][...]

    slots = levels // vox
    owners = [choose(o, z, p, slots, levels)[0] + o * slots for o in range(vox) for p in phases]
    needed = functools.reduce(jnp.logical_or, [at <= z for at in owners])

    @pl.when(jnp.logical_not(needed))
    def _():
        for out in outs:
            out[...] = jnp.zeros_like(out)

    @pl.when(needed)
    def _():
        for i in range(len(near)):
            total = 0.0
            for part in (high_ref, low_ref):
                total += lax.dot_general(
                    part[i], cols_ref[i], (((1,), (1,)), ((), ())), preferred_element_type=jnp.float32
                )
            for n, (t, p) in enumerate(parts):
                to = (p * len(near) + i) * tile
                for j in range(len(far)):
                    outs[t * len(far) + j][:tile, to : to + tile] = total[
                        j * tile : (j + 1) * tile, n * tile : (n + 1) * tile
                    ]
        for out in outs[1:]:
            largest = jnp.max(jnp.abs(out[:tile]), axis=(0, 1), keepdims=True)
            power = jnp.floor(jnp.log2(jnp.maximum(largest, 1e-30))) - 13.0
            out[:tile] *= jnp.exp2(-power)
            out[tile:] = jnp.broadcast_to(power, out[tile:].shape)


def multiply(high, low, pieces, levels, vox, phases, far, near):
    tile, depth = pieces[0][0].shape
    dists = sorted(set().union(*[used(p, levels // vox, levels) for p in phases]))
    flat = [pieces[d][i] for d in dists for i in range(len(near))]
    heights = [tile] + [tile + EXTRA] * (vox * len(far) - 1)
    width = len(phases) * len(near) * tile
    call = kernel_call(
        functools.partial(multiply_kernel, vox, levels, phases, dists, far, near),
        [VMEM] * (2 + len(flat)),
        [jax.ShapeDtypeStruct((height, width), jnp.float32) for height in heights],
        [pltpu.VMEM((len(near), vox * len(phases) * tile, depth), jnp.bfloat16)],
    )
    return call(high, low, *flat)


def place_kernel(vox, levels, lines, groups, far, near, *refs):
    perm = [7, 6, 5, 4, 3, 1, 2, 0] if len(refs) == 9 else range(len(refs) - 1)
    blocks, out_ref = [refs[list(perm).index(k)] for k in range(len(refs) - 1)], refs[-1]
    tile, slots = out_ref.shape[0], levels // vox
    v, z, w = (lax.axis_index(a) for a in ("vox", "row", "wl"))
    rows = (z * lines + w) * tile + lax.broadcasted_iota(jnp.int32, (tile, tile), 0)
    for g, phases in enumerate(groups):
        for p, phase in enumerate(phases):
            slot, _ = choose(v, z, phase, slots, levels)
            for j, f in enumerate(far):
                for i, e in enumerate(near):
                    src = slice((p * len(near) + i) * tile, (p * len(near) + i + 1) * tile)
                    total = 0.0
                    for t in range(vox):
                        block = blocks[(g * vox + t) * len(far) + j]
                        scale = 1.0 if t == j == 0 else jnp.exp2(block[tile : tile + 1, :1])
                        total += block[:tile, src] * scale
                    at = pl.multiple_of((slot * lines + (w ^ f ^ e)) * tile, tile)
                    cols = v * (slots * lines * tile) + at + lax.broadcasted_iota(jnp.int32, (tile, tile), 1)
                    out_ref[:, pl.ds(at, tile)] = jnp.where(cols <= rows, total, 0.0)


def place(blocks, vox, levels, lines, groups, far, near):
    tile = blocks[0].shape[0]
    call = kernel_call(
        functools.partial(place_kernel, vox, levels, lines, groups, far, near),
        [VMEM] * len(blocks),
        [jax.ShapeDtypeStruct((tile, levels // vox * lines * tile), jnp.float32)],
    )
    perm = [7, 6, 5, 4, 3, 1, 2, 0] if len(blocks) == 8 else range(len(blocks))
    return call(*[blocks[k] for k in perm])[0]


def on_device(jac, extinction, prior_var):
    vox, levels, lines = (lax.axis_size(a) for a in ("vox", "row", "wl"))
    tile, slots = jac.shape[0], levels // vox
    far = [0, lines // 2] if lines > 1 else [0]
    near = list(range(max(lines // 2, 1)))

    groups = [[p] for p in range(slots)]

    below = {0: jac}
    if levels > 1:
        below[1] = shift(jac, "row", 1)
    others = [swap(jac, "wl", f) for f in far[1:]]
    if levels > 2:
        below[levels - 1] = climb(jac, levels - 1, levels - 1, 1)
    weights, own = prepare(extinction.T, prior_var, jac, far, near)
    if levels > 1:
        below[1], weights, own = lax.optimization_barrier([below[1], weights, own])
    for d in range(2, levels - 1):
        below[d] = climb(below[d - 1], 1, d, levels - d)
    high, low = weigh(weights, [own] + others, far, near)
    below[0] = own

    def both(d):
        n = {0: 1, 1: 2}.get(d, 2)
        cuts = [below[d][k * tile // n : (k + 1) * tile // n] for k in range(n)]
        swapped = [[swap(x, "wl", e) for x in cuts] for e in near[1:]]
        return [below[d]] + [jnp.concatenate(xs, axis=0) if len(xs) > 1 else xs[0] for xs in swapped]

    pieces = {d: both(d) for d in (0, 1, levels - 1)}
    blocks = []
    for phases in groups:
        dists = sorted(set().union(*[used(p, slots, levels) for p in phases]))
        late = [d for d in dists if d not in pieces]
        if late:
            flat = lax.optimization_barrier([below[d] for d in late] + blocks)
            blocks = list(flat[len(late) :])
            for d, x in zip(late, flat):
                pieces[d] = [x] + [swap(x, "wl", e) for e in near[1:]]
        shares = multiply(high, low, pieces, levels, vox, phases, far, near)
        blocks += [share.astype(jnp.float16) if k else share for k, share in enumerate(shares)]
    sent = []
    for k, share in enumerate(blocks):
        t, j = divmod(k % (vox * len(far)), len(far))
        sent.append(send(share, t, far[j]).astype(jnp.float32) if t or j else share)
    return place(sent, vox, levels, lines, groups, far, near)


def solution(mesh):
    return jax.shard_map(
        on_device,
        mesh=mesh,
        in_specs=(P(("row", "wl"), "vox"), P(), P(None, "vox")),
        out_specs=P(("row", "wl"), "vox"),
        check_vma=False,
    )
```
